32 devices in a mesh: tm: 2 (over x), space: 16 (over z, y, core).
Axes of the slice: x: 2, y: 2, z: 4, core: 2. Of those that a mesh axis runs over, the one named last changes fastest.
Arguments:
- states: float32 [2, 3, 32, 128, 128], P('tm', None, 'space'), may hold values from -2 to 2
- viscosity: float32 [32, 128, 128], P('space'), may hold values from 0.2 to 0.6
Outputs:
- corrected: float32 [2, 3, 32, 128, 128], P('tm', None, 'space')
The draws below stay inside these ranges and needn't reach their ends.
All inputs are finite; a program needn't handle non-finite values.
Results may differ from the reference program's by a relative error of at most 0.00002.
Values sent between devices are 32-bit elements; how exact they have to be, the bound alone decides.
A program may use at most 64 MiB of HBM per device.

```python
import math
import jax
import jax.numpy as jnp

NY = 128
NX = 128
GROUPS = 2
NZ = 32


def draw_states(key, part):
    key = jax.random.fold_in(key, 7)
    shape = (GROUPS, 3, NZ, NY, NX)
    values = 0.5 * jax.random.normal(key, shape, jnp.float32)
    return jnp.clip(values, -2.0, 2.0)


def shard_levels(rng, shape, cuts, smallest, high):
    loudness, own = 1.0, jax.random.fold_in(rng, 6)
    for position, blocks in cuts:
        steps = jnp.exp(jax.random.uniform(jax.random.fold_in(own, position), (blocks,), jnp.float32, smallest / len(cuts), high / len(cuts)))
        loudness = loudness * jnp.repeat(steps, shape[position] // blocks).reshape([-1 if axis == position else 1 for axis in range(len(shape))])
    return loudness


def setup_inputs(seed: int = 0) -> dict:
    seeds = jax.random.split(jax.random.key(seed), 3)
    states = draw_states(jax.random.fold_in(seeds[2], 71), 0)
    viscosity = jnp.clip(jnp.exp(math.log(0.6) - 1.0986123 * jax.random.uniform(seeds[1], (NZ, NY, NX), jnp.float32) ** shard_levels(seeds[1], (NZ, NY, NX), ((0, 16),), -0.2, 0.2)), 0.2, 0.6)
    return dict(states=states, viscosity=viscosity)


FINE_STEP = 0.12
COARSE_STEP = 0.24


def advance(center, above, below, visc, step):
    y_plus = jnp.roll(center, -1, axis=-2)
    y_minus = jnp.roll(center, 1, axis=-2)
    x_plus = jnp.roll(center, -1, axis=-1)
    x_minus = jnp.roll(center, 1, axis=-1)
    laplace = (above + below) + (y_plus + y_minus) + (x_plus + x_minus) - 6.0 * center
    carried = center[0:1] * (above - below) * 0.5 + center[1:2] * (y_plus - y_minus) * 0.5 + center[2:3] * (x_plus - x_minus) * 0.5
    return center + step * (visc[None] * laplace - carried)


def whole_step(field, visc, step):
    return advance(field, jnp.roll(field, -1, axis=1), jnp.roll(field, 1, axis=1), visc, step)


def reference(states, viscosity):
    jumps = []
    for group in range(GROUPS):
        own = states[group]
        fine = whole_step(whole_step(own, viscosity, FINE_STEP), viscosity, FINE_STEP)
        jumps.append(fine - whole_step(own, viscosity, COARSE_STEP))
    start = states[0]
    results = []
    for group in range(GROUPS):
        start = whole_step(start, viscosity, COARSE_STEP) + jumps[group]
        results.append(start)
    return jnp.stack(results, axis=0)
```

```python
import functools

import jax
import jax.numpy as jnp
from jax import lax
from jax.experimental import pallas as pl
from jax.experimental.pallas import tpu as pltpu
from jax.sharding import PartitionSpec as P

FINE_STEP = 0.12
COARSE_STEP = 0.24
MESH = pl.DeviceIdType.MESH
TILE = 8


def row_plan(tiles):
    cuts = [0] + [max(1, tiles * part // 16) for part in (6, 10, 14)] + [tiles]
    chunks = [(a, b) for a, b in zip(cuts, cuts[1:]) if b > a]
    fine_one, fine_two = [], []
    done_one, done_two = 1, 2
    for _, end in chunks:
        last = end == tiles
        upto_one = tiles + 1 if last else max(done_one, end - 1)
        upto_two = tiles + 2 if last else max(done_two, end - 2)
        fine_one.append((done_one, upto_one))
        fine_two.append((done_two, upto_two))
        done_one, done_two = upto_one, upto_two
    return chunks, fine_one, fine_two


def pieces_of(first, last, tiles):
    pieces = []
    if first < min(last, tiles):
        pieces.append((first, min(last, tiles)))
    if last > tiles:
        pieces.append((max(first, tiles) - tiles, last - tiles))
    return pieces


def rates(ref, plane, row, visc, nx):
    center = [ref[c, plane, pl.ds(row, TILE), :] for c in range(3)]
    out = []
    for c in range(3):
        u = center[c]
        above = ref[c, plane + 1, pl.ds(row, TILE), :]
        below = ref[c, plane - 1, pl.ds(row, TILE), :]
        y_plus = ref[c, plane, pl.ds(row + 1, TILE), :]
        y_minus = ref[c, plane, pl.ds(row - 1, TILE), :]
        x_plus = pltpu.roll(u, nx - 1, 1)
        x_minus = pltpu.roll(u, 1, 1)
        laplace = (above + below) + (y_plus + y_minus) + (x_plus + x_minus) - 6.0 * u
        carried = (
            center[0] * (above - below)
            + center[1] * (y_plus - y_minus)
            + center[2] * (x_plus - x_minus)
        )
        out.append(visc * laplace - 0.5 * carried)
    return center, out


def kernel(
    count, groups, states, viscosity, result,
    field, visc, fine, jump, start,
    own_sem, send_s, recv_s, send_v, recv_v, send_c, recv_c, send_h, recv_h,
):
    _, _, nz, ny, nx = states.shape
    tiles = ny // TILE
    chunks, fine_one, fine_two = row_plan(tiles)
    pieces = [pieces_of(first, last, tiles) for first, last in fine_two]
    numbered, serial = [], 0
    for group in pieces:
        numbered.append([(serial + k, a, b) for k, (a, b) in enumerate(group)])
        serial += len(group)

    me = lax.axis_index("space")
    turn = lax.axis_index("tm")
    right = lax.rem(me + 1, count)
    left = lax.rem(me + count - 1, count)

    own_state = pltpu.make_async_copy(
        states.at[0], field.at[:, pl.ds(2, nz), pl.ds(TILE, ny), :], own_sem.at[0])
    own_visc = pltpu.make_async_copy(viscosity, visc.at[pl.ds(1, nz)], own_sem.at[1])
    own_state.start()
    own_visc.start()

    def next_turn():
        return {"tm": turn + 1}

    barrier = pltpu.get_barrier_semaphore()
    for side in (left, right):
        pl.semaphore_signal(barrier, inc=1, device_id={"space": side}, device_id_type=MESH)
    if groups > 1:
        @pl.when(turn > 0)
        def _():
            pl.semaphore_signal(barrier, inc=1, device_id={"tm": turn - 1}, device_id_type=MESH)

        @pl.when(turn < groups - 1)
        def _():
            pl.semaphore_signal(barrier, inc=1, device_id=next_turn(), device_id_type=MESH)

    peers = 2 + (turn > 0).astype(jnp.int32) + (turn < groups - 1).astype(jnp.int32)
    pl.semaphore_wait(barrier, peers)

    def halo_copies(k):
        first, last = chunks[k]
        rows = pl.ds(first * TILE, (last - first) * TILE)
        padded = pl.ds((first + 1) * TILE, (last - first) * TILE)
        copies = []
        for d, (side, src, dst, vsrc, vdst) in enumerate((
            (right, nz - 2, 0, nz - 1, 0),
            (left, 0, nz + 2, 0, nz + 1),
        )):
            copies.append(pltpu.make_async_remote_copy(
                viscosity.at[vsrc, rows, :], visc.at[vdst, rows, :],
                send_v.at[d, k], recv_v.at[d, k],
                device_id={"space": side}, device_id_type=MESH))
            copies.append(pltpu.make_async_remote_copy(
                states.at[0, :, pl.ds(src, 2), rows, :], field.at[:, pl.ds(dst, 2), padded, :],
                send_s.at[d, k], recv_s.at[d, k],
                device_id={"space": side}, device_id_type=MESH))
        return copies

    def pass_copy(i, a, b):
        rows = pl.ds(a * TILE, (b - a) * TILE)
        padded = pl.ds((a + 1) * TILE, (b - a) * TILE)
        return pltpu.make_async_remote_copy(
            result.at[0, :, :, rows, :], start.at[:, pl.ds(1, nz), padded, :],
            send_c.at[i], recv_c.at[i], device_id=next_turn(), device_id_type=MESH)

    def edge_copies(i, a, b):
        padded = pl.ds((a + 1) * TILE, (b - a) * TILE)
        return [
            pltpu.make_async_remote_copy(
                start.at[:, src, padded, :], start.at[:, dst, padded, :],
                send_h.at[d, i], recv_h.at[d, i],
                device_id={"space": side}, device_id_type=MESH)
            for d, (side, src, dst) in enumerate(((right, nz, 0), (left, 1, nz + 1)))
        ]

    halos = [halo_copies(k) for k in range(len(chunks))]
    for copies in halos:
        for copy in copies:
            copy.start()
    own_state.wait()
    own_visc.wait()

    def wrap_rows(ref):
        for c in range(3):
            for plane in range(ref.shape[1]):
                ref[c, plane, pl.ds(TILE - 1, 1), :] = ref[c, plane, pl.ds(TILE + ny - 1, 1), :]
                ref[c, plane, pl.ds(TILE + ny, 1), :] = ref[c, plane, pl.ds(TILE, 1), :]

    def first_step(t, _):
        row = lax.rem(t, tiles) * TILE
        for plane in range(nz + 2):
            here, rate = rates(field, plane + 1, row + TILE, visc[plane, pl.ds(row, TILE), :], nx)
            for c in range(3):
                fine[c, plane, pl.ds(row + TILE, TILE), :] = here[c] + FINE_STEP * rate[c]
                if 1 <= plane <= nz:
                    jump[c, plane - 1, pl.ds(row, TILE), :] = here[c] + COARSE_STEP * rate[c]
        return _

    def second_step(t, _):
        row = lax.rem(t, tiles) * TILE
        for plane in range(nz):
            here, rate = rates(
                fine, plane + 1, row + TILE, visc[plane + 1, pl.ds(row, TILE), :], nx)
            for c in range(3):
                coarse = jump[c, plane, pl.ds(row, TILE), :]
                change = here[c] + FINE_STEP * rate[c] - coarse
                jump[c, plane, pl.ds(row, TILE), :] = change
                result[0, c, plane, pl.ds(row, TILE), :] = coarse + change
        return _

    def correct(t, _):
        row = t * TILE
        for plane in range(nz):
            here, rate = rates(
                start, plane + 1, row + TILE, visc[plane + 1, pl.ds(row, TILE), :], nx)
            for c in range(3):
                result[0, c, plane, pl.ds(row, TILE), :] = (
                    here[c] + COARSE_STEP * rate[c] + jump[c, plane, pl.ds(row, TILE), :])
        return _

    def hand_on(group):
        if groups > 1 and group:
            @pl.when(turn == 0)
            def _():
                for piece in group:
                    pass_copy(*piece).start()

    def take_over(group):
        if groups > 1 and group:
            @pl.when(turn > 0)
            def _():
                for piece in group:
                    pass_copy(*piece).wait_recv()
                    for copy in edge_copies(*piece):
                        copy.start()

    for k in range(len(chunks)):
        for copy in halos[k]:
            copy.wait_recv()
        last = k == len(chunks) - 1
        if last:
            wrap_rows(field)
        lax.fori_loop(*fine_one[k], first_step, None)
        if last:
            wrap_rows(fine)
        lax.fori_loop(*fine_two[k], second_step, None)
        hand_on(numbered[k])
        if groups == 2 and k > 0:
            take_over(numbered[k - 1])

    if groups > 1:
        @pl.when(turn > 0)
        def _():
            for k in range(len(chunks)):
                if groups > 2 or k == len(chunks) - 1:
                    for piece in numbered[k]:
                        pass_copy(*piece).wait_recv()
                        for copy in edge_copies(*piece):
                            copy.start()
            for group in numbered:
                for piece in group:
                    for copy in edge_copies(*piece):
                        copy.wait_recv()
            wrap_rows(start)
            lax.fori_loop(0, tiles, correct, None)

            @pl.when(turn < groups - 1)
            def _():
                for group in numbered:
                    for piece in group:
                        pass_copy(*piece).start()

            for group in numbered:
                for piece in group:
                    for copy in edge_copies(*piece):
                        copy.wait_send()

        @pl.when(turn < groups - 1)
        def _():
            for group in numbered:
                for piece in group:
                    pass_copy(*piece).wait_send()

    for copies in halos:
        for copy in copies:
            copy.wait_send()


def local(count, groups, states, viscosity):
    _, _, nz, ny, nx = states.shape
    chunks, _, fine_two = row_plan(ny // TILE)
    passes = sum(len(pieces_of(a, b, ny // TILE)) for a, b in fine_two)
    padded = ny + 2 * TILE
    f32 = jnp.float32
    dma = pltpu.SemaphoreType.DMA
    return pl.pallas_call(
        functools.partial(kernel, count, groups),
        out_shape=jax.ShapeDtypeStruct(states.shape, f32),
        in_specs=[pl.BlockSpec(memory_space=pl.ANY)] * 2,
        out_specs=pl.BlockSpec(memory_space=pltpu.VMEM),
        scratch_shapes=[
            pltpu.VMEM((3, nz + 4, padded, nx), f32),
            pltpu.VMEM((nz + 2, ny, nx), f32),
            pltpu.VMEM((3, nz + 2, padded, nx), f32),
            pltpu.VMEM((3, nz, ny, nx), f32),
            pltpu.VMEM((3, nz + 2, padded, nx), f32),
            dma((2,)),
            dma((2, len(chunks))),
            dma((2, len(chunks))),
            dma((2, len(chunks))),
            dma((2, len(chunks))),
            dma((passes,)),
            dma((passes,)),
            dma((2, passes)),
            dma((2, passes)),
        ],
        compiler_params=pltpu.CompilerParams(
            collective_id=0, has_side_effects=True, vmem_limit_bytes=32 * 1024 * 1024),
    )(states, viscosity)


def solution(mesh):
    return jax.shard_map(
        functools.partial(local, mesh.shape["space"], mesh.shape["tm"]),
        mesh=mesh,
        in_specs=(P("tm", None, "space", None, None), P("space", None, None)),
        out_specs=P("tm", None, "space", None, None),
        check_vma=False,
    )
```

```python
import functools

import jax
import jax.numpy as jnp
from jax import lax
from jax.experimental import pallas as pl
from jax.experimental.pallas import tpu as pltpu
from jax.sharding import PartitionSpec as P

FINE_STEP = 0.12
COARSE_STEP = 0.24
MESH = pl.DeviceIdType.MESH
TILE = 8
MOST = 4
UNROLL = 2


def row_plan(tiles):
    cuts = [0] + [max(1, tiles * part // 16) for part in (6, 10, 14)] + [tiles]
    chunks = [(a, b) for a, b in zip(cuts, cuts[1:]) if b > a]
    fine_one, fine_two = [], []
    done_one, done_two = 1, 2
    for _, end in chunks:
        last = end == tiles
        upto_one = tiles + 1 if last else max(done_one, end - 1)
        upto_two = tiles + 2 if last else max(done_two, end - 2)
        fine_one.append((done_one, upto_one))
        fine_two.append((done_two, upto_two))
        done_one, done_two = upto_one, upto_two
    return chunks, fine_one, fine_two


def pieces_of(first, last, tiles):
    pieces = []
    while first < last:
        begin = first % tiles
        length = min(MOST, last - first, tiles - begin)
        pieces.append((begin, begin + length))
        first += length
    return pieces


def rates(ref, plane, row, visc, nx):
    center = [ref[c, plane, pl.ds(row, TILE), :] for c in range(3)]
    out = []
    for c in range(3):
        u = center[c]
        above = ref[c, plane + 1, pl.ds(row, TILE), :]
        below = ref[c, plane - 1, pl.ds(row, TILE), :]
        y_plus = ref[c, plane, pl.ds(row + 1, TILE), :]
        y_minus = ref[c, plane, pl.ds(row - 1, TILE), :]
        x_plus = pltpu.roll(u, nx - 1, 1)
        x_minus = pltpu.roll(u, 1, 1)
        laplace = (above + below) + (y_plus + y_minus) + (x_plus + x_minus) - 6.0 * u
        carried = (
            center[0] * (above - below)
            + center[1] * (y_plus - y_minus)
            + center[2] * (x_plus - x_minus)
        )
        out.append(visc * laplace - 0.5 * carried)
    return center, out


def kernel(
    count, groups, states, viscosity, result,
    field, visc, fine, jump, start,
    own_sem, send_s, recv_s, send_v, recv_v, send_c, recv_c, send_h, recv_h,
):
    _, _, nz, ny, nx = states.shape
    tiles = ny // TILE
    chunks, fine_one, fine_two = row_plan(tiles)
    pieces = [pieces_of(first, last, tiles) for first, last in fine_two]
    numbered, serial = [], 0
    for group in pieces:
        numbered.append([(serial + k, a, b) for k, (a, b) in enumerate(group)])
        serial += len(group)

    me = lax.axis_index("space")
    turn = lax.axis_index("tm")
    right = lax.rem(me + 1, count)
    left = lax.rem(me + count - 1, count)

    own_state = pltpu.make_async_copy(
        states.at[0], field.at[:, pl.ds(2, nz), pl.ds(TILE, ny), :], own_sem.at[0])
    own_visc = pltpu.make_async_copy(viscosity, visc.at[pl.ds(1, nz)], own_sem.at[1])
    own_state.start()
    own_visc.start()

    def next_turn():
        return {"tm": turn + 1}

    barrier = pltpu.get_barrier_semaphore()
    for side in (left, right):
        pl.semaphore_signal(barrier, inc=1, device_id={"space": side}, device_id_type=MESH)
    if groups > 1:
        @pl.when(turn > 0)
        def _():
            pl.semaphore_signal(barrier, inc=1, device_id={"tm": turn - 1}, device_id_type=MESH)

        @pl.when(turn < groups - 1)
        def _():
            pl.semaphore_signal(barrier, inc=1, device_id=next_turn(), device_id_type=MESH)

    peers = 2 + (turn > 0).astype(jnp.int32) + (turn < groups - 1).astype(jnp.int32)
    pl.semaphore_wait(barrier, peers)

    def halo_copies(k):
        first, last = chunks[k]
        rows = pl.ds(first * TILE, (last - first) * TILE)
        padded = pl.ds((first + 1) * TILE, (last - first) * TILE)
        copies = []
        for d, (side, src, dst, vsrc, vdst) in enumerate((
            (right, nz - 2, 0, nz - 1, 0),
            (left, 0, nz + 2, 0, nz + 1),
        )):
            copies.append(pltpu.make_async_remote_copy(
                viscosity.at[vsrc, rows, :], visc.at[vdst, rows, :],
                send_v.at[d, k], recv_v.at[d, k],
                device_id={"space": side}, device_id_type=MESH))
            copies.append(pltpu.make_async_remote_copy(
                states.at[0, :, pl.ds(src, 2), rows, :], field.at[:, pl.ds(dst, 2), padded, :],
                send_s.at[d, k], recv_s.at[d, k],
                device_id={"space": side}, device_id_type=MESH))
        return copies

    def pass_copy(i, a, b):
        rows = pl.ds(a * TILE, (b - a) * TILE)
        padded = pl.ds((a + 1) * TILE, (b - a) * TILE)
        return pltpu.make_async_remote_copy(
            result.at[0, :, :, rows, :], start.at[:, pl.ds(1, nz), padded, :],
            send_c.at[i], recv_c.at[i], device_id=next_turn(), device_id_type=MESH)

    def edge_copies(i, a, b):
        padded = pl.ds((a + 1) * TILE, (b - a) * TILE)
        return [
            pltpu.make_async_remote_copy(
                start.at[:, src, padded, :], start.at[:, dst, padded, :],
                send_h.at[d, i], recv_h.at[d, i],
                device_id={"space": side}, device_id_type=MESH)
            for d, (side, src, dst) in enumerate(((right, nz, 0), (left, 1, nz + 1)))
        ]

    halos = [halo_copies(k) for k in range(len(chunks))]
    for copies in halos:
        for copy in copies:
            copy.start()
    own_state.wait()
    own_visc.wait()

    def wrap_rows(ref):
        for c in range(3):
            for plane in range(ref.shape[1]):
                ref[c, plane, pl.ds(TILE - 1, 1), :] = ref[c, plane, pl.ds(TILE + ny - 1, 1), :]
                ref[c, plane, pl.ds(TILE + ny, 1), :] = ref[c, plane, pl.ds(TILE, 1), :]

    def first_step(t, _):
        row = lax.rem(t, tiles) * TILE
        for plane in range(nz + 2):
            here, rate = rates(field, plane + 1, row + TILE, visc[plane, pl.ds(row, TILE), :], nx)
            for c in range(3):
                fine[c, plane, pl.ds(row + TILE, TILE), :] = here[c] + FINE_STEP * rate[c]
                if 1 <= plane <= nz:
                    jump[c, plane - 1, pl.ds(row, TILE), :] = here[c] + COARSE_STEP * rate[c]
        return _

    def second_step(t, _):
        row = lax.rem(t, tiles) * TILE
        for plane in range(nz):
            here, rate = rates(
                fine, plane + 1, row + TILE, visc[plane + 1, pl.ds(row, TILE), :], nx)
            for c in range(3):
                coarse = jump[c, plane, pl.ds(row, TILE), :]
                change = here[c] + FINE_STEP * rate[c] - coarse
                jump[c, plane, pl.ds(row, TILE), :] = change
                result[0, c, plane, pl.ds(row, TILE), :] = coarse + change
        return _

    def correct(t, _):
        row = lax.rem(t, tiles) * TILE
        for plane in range(nz):
            here, rate = rates(
                start, plane + 1, row + TILE, visc[plane + 1, pl.ds(row, TILE), :], nx)
            for c in range(3):
                result[0, c, plane, pl.ds(row, TILE), :] = (
                    here[c] + COARSE_STEP * rate[c] + jump[c, plane, pl.ds(row, TILE), :])
        return _

    def hand_on(group):
        if groups > 1 and group:
            @pl.when(turn == 0)
            def _():
                for piece in group:
                    pass_copy(*piece).start()

    def take_over(group):
        if groups > 1 and group:
            @pl.when(turn > 0)
            def _():
                for piece in group:
                    pass_copy(*piece).wait_recv()
                    for copy in edge_copies(*piece):
                        copy.start()

    for k in range(len(chunks)):
        for copy in halos[k]:
            copy.wait_recv()
        last = k == len(chunks) - 1
        if last:
            wrap_rows(field)
        lax.fori_loop(*fine_one[k], first_step, None, unroll=UNROLL)
        if last:
            wrap_rows(fine)
        for piece in numbered[k]:
            lax.fori_loop(piece[1], piece[2], second_step, None, unroll=UNROLL)
            hand_on([piece])
        if groups == 2 and k > 0:
            take_over(numbered[k - 1])

    if groups > 1:
        @pl.when(turn > 0)
        def _():
            for k in range(len(chunks)):
                if groups > 2 or k == len(chunks) - 1:
                    for piece in numbered[k]:
                        pass_copy(*piece).wait_recv()
                        for copy in edge_copies(*piece):
                            copy.start()
            done = 3
            for (_, upto), group in zip(fine_two, numbered):
                for piece in group:
                    for copy in edge_copies(*piece):
                        copy.wait_recv()
                upto = upto + 1 if upto > tiles else upto - 1
                if upto > tiles:
                    wrap_rows(start)
                if upto > done:
                    lax.fori_loop(done, upto, correct, None, unroll=UNROLL)
                    done = upto

            @pl.when(turn < groups - 1)
            def _():
                for group in numbered:
                    for piece in group:
                        pass_copy(*piece).start()

            for group in numbered:
                for piece in group:
                    for copy in edge_copies(*piece):
                        copy.wait_send()

        @pl.when(turn < groups - 1)
        def _():
            for group in numbered:
                for piece in group:
                    pass_copy(*piece).wait_send()

    for copies in halos:
        for copy in copies:
            copy.wait_send()


def local(count, groups, states, viscosity):
    _, _, nz, ny, nx = states.shape
    chunks, _, fine_two = row_plan(ny // TILE)
    passes = sum(len(pieces_of(a, b, ny // TILE)) for a, b in fine_two)
    padded = ny + 2 * TILE
    f32 = jnp.float32
    dma = pltpu.SemaphoreType.DMA
    return pl.pallas_call(
        functools.partial(kernel, count, groups),
        out_shape=pltpu.VMEM(states.shape, f32),
        in_specs=[pl.BlockSpec(memory_space=pl.ANY)] * 2,
        out_specs=pl.BlockSpec(memory_space=pltpu.VMEM),
        scratch_shapes=[
            pltpu.VMEM((3, nz + 4, padded, nx), f32),
            pltpu.VMEM((nz + 2, ny, nx), f32),
            pltpu.VMEM((3, nz + 2, padded, nx), f32),
            pltpu.VMEM((3, nz, ny, nx), f32),
            pltpu.VMEM((3, nz + 2, padded, nx), f32),
            dma((2,)),
            dma((2, len(chunks))),
            dma((2, len(chunks))),
            dma((2, len(chunks))),
            dma((2, len(chunks))),
            dma((passes,)),
            dma((passes,)),
            dma((2, passes)),
            dma((2, passes)),
        ],
        compiler_params=pltpu.CompilerParams(
            collective_id=0, has_side_effects=True),
    )(
        pltpu.with_memory_space_constraint(states, pltpu.HBM),
        pltpu.with_memory_space_constraint(viscosity, pltpu.HBM),
    )


def solution(mesh):
    return jax.shard_map(
        functools.partial(local, mesh.shape["space"], mesh.shape["tm"]),
        mesh=mesh,
        in_specs=(P("tm", None, "space", None, None), P("space", None, None)),
        out_specs=P("tm", None, "space", None, None),
        check_vma=False,
    )
```

```python
import functools

import jax
import jax.numpy as jnp
from jax import lax
from jax.experimental import pallas as pl
from jax.experimental.pallas import tpu as pltpu
from jax.sharding import PartitionSpec as P

FINE_STEP = 0.12
COARSE_STEP = 0.24
MESH = pl.DeviceIdType.MESH
TILE = 8
MOST = 4
UNROLL = 2


def row_plan(tiles):
    cuts = [0] + [max(1, tiles * part // 16) for part in (5, 8, 11, 14)] + [tiles]
    chunks = [(a, b) for a, b in zip(cuts, cuts[1:]) if b > a]
    fine_one, fine_two = [], []
    done_one, done_two = 1, 2
    for _, end in chunks:
        last = end == tiles
        upto_one = tiles + 1 if last else max(done_one, end - 1)
        upto_two = tiles + 2 if last else max(done_two, end - 2)
        fine_one.append((done_one, upto_one))
        fine_two.append((done_two, upto_two))
        done_one, done_two = upto_one, upto_two
    return chunks, fine_one, fine_two


def pieces_of(first, last, tiles):
    pieces = []
    while first < last:
        begin = first % tiles
        length = min(MOST, last - first, tiles - begin)
        pieces.append((begin, begin + length))
        first += length
    return pieces


def rates(ref, plane, row, visc, nx):
    center = [ref[c, plane, pl.ds(row, TILE), :] for c in range(3)]
    out = []
    for c in range(3):
        u = center[c]
        above = ref[c, plane + 1, pl.ds(row, TILE), :]
        below = ref[c, plane - 1, pl.ds(row, TILE), :]
        y_plus = ref[c, plane, pl.ds(row + 1, TILE), :]
        y_minus = ref[c, plane, pl.ds(row - 1, TILE), :]
        x_plus = pltpu.roll(u, nx - 1, 1)
        x_minus = pltpu.roll(u, 1, 1)
        laplace = (above + below) + (y_plus + y_minus) + (x_plus + x_minus) - 6.0 * u
        carried = (
            center[0] * (above - below)
            + center[1] * (y_plus - y_minus)
            + center[2] * (x_plus - x_minus)
        )
        out.append(visc * laplace - 0.5 * carried)
    return center, out


def kernel(
    count, groups, states, viscosity, result,
    field, visc, fine, jump, start,
    own_sem, send_s, recv_s, send_v, recv_v, send_c, recv_c, send_h, recv_h,
):
    _, _, nz, ny, nx = states.shape
    tiles = ny // TILE
    chunks, fine_one, fine_two = row_plan(tiles)
    pieces = [pieces_of(first, last, tiles) for first, last in fine_two]
    numbered, serial = [], 0
    for group in pieces:
        numbered.append([(serial + k, a, b) for k, (a, b) in enumerate(group)])
        serial += len(group)

    me = lax.axis_index("space")
    turn = lax.axis_index("tm")
    right = lax.rem(me + 1, count)
    left = lax.rem(me + count - 1, count)
    odd = lax.rem(me, 2)

    own_state = pltpu.make_async_copy(
        states.at[0], field.at[:, pl.ds(2, nz), pl.ds(TILE, ny), :], own_sem.at[0])
    own_visc = pltpu.make_async_copy(viscosity, visc.at[pl.ds(1, nz)], own_sem.at[1])
    own_state.start()
    own_visc.start()

    def next_turn():
        return {"tm": turn + 1}

    barrier = pltpu.get_barrier_semaphore()
    for side in (left, right):
        pl.semaphore_signal(barrier, inc=1, device_id={"space": side}, device_id_type=MESH)
    if groups > 1:
        @pl.when(turn > 0)
        def _():
            pl.semaphore_signal(barrier, inc=1, device_id={"tm": turn - 1}, device_id_type=MESH)

        @pl.when(turn < groups - 1)
        def _():
            pl.semaphore_signal(barrier, inc=1, device_id=next_turn(), device_id_type=MESH)

    peers = 2 + (turn > 0).astype(jnp.int32) + (turn < groups - 1).astype(jnp.int32)
    pl.semaphore_wait(barrier, peers)

    def halo_copies(k):
        first, last = chunks[k]
        rows = pl.ds(first * TILE, (last - first) * TILE)
        padded = pl.ds((first + 1) * TILE, (last - first) * TILE)
        copies = []
        for d in (1 - odd, odd):
            side = lax.rem(me + 1 + d * (count - 2), count)
            src, dst = (1 - d) * (nz - 2), d * (nz + 2)
            vsrc, vdst = (1 - d) * (nz - 1), d * (nz + 1)
            copies.append(pltpu.make_async_remote_copy(
                viscosity.at[vsrc, rows, :], visc.at[vdst, rows, :],
                send_v.at[d, k], recv_v.at[d, k],
                device_id={"space": side}, device_id_type=MESH))
            copies.append(pltpu.make_async_remote_copy(
                states.at[0, :, pl.ds(src, 2), rows, :], field.at[:, pl.ds(dst, 2), padded, :],
                send_s.at[d, k], recv_s.at[d, k],
                device_id={"space": side}, device_id_type=MESH))
        return copies

    def pass_copy(i, a, b):
        rows = pl.ds(a * TILE, (b - a) * TILE)
        padded = pl.ds((a + 1) * TILE, (b - a) * TILE)
        return pltpu.make_async_remote_copy(
            result.at[0, :, :, rows, :], start.at[:, pl.ds(1, nz), padded, :],
            send_c.at[i], recv_c.at[i], device_id=next_turn(), device_id_type=MESH)

    def edge_copies(i, a, b):
        padded = pl.ds((a + 1) * TILE, (b - a) * TILE)
        return [
            pltpu.make_async_remote_copy(
                start.at[:, src, padded, :], start.at[:, dst, padded, :],
                send_h.at[d, i], recv_h.at[d, i],
                device_id={"space": side}, device_id_type=MESH)
            for d, (side, src, dst) in enumerate(((right, nz, 0), (left, 1, nz + 1)))
        ]

    halos = [halo_copies(k) for k in range(len(chunks))]
    for copies in halos:
        for copy in copies:
            copy.start()
    own_state.wait()
    own_visc.wait()

    def wrap_rows(ref):
        for c in range(3):
            for plane in range(ref.shape[1]):
                ref[c, plane, pl.ds(TILE - 1, 1), :] = ref[c, plane, pl.ds(TILE + ny - 1, 1), :]
                ref[c, plane, pl.ds(TILE + ny, 1), :] = ref[c, plane, pl.ds(TILE, 1), :]

    def first_step(t, _):
        row = lax.rem(t, tiles) * TILE
        for plane in range(nz + 2):
            here, rate = rates(field, plane + 1, row + TILE, visc[plane, pl.ds(row, TILE), :], nx)
            for c in range(3):
                fine[c, plane, pl.ds(row + TILE, TILE), :] = here[c] + FINE_STEP * rate[c]
                if 1 <= plane <= nz:
                    jump[c, plane - 1, pl.ds(row, TILE), :] = here[c] + COARSE_STEP * rate[c]
        return _

    def second_step(t, _):
        row = lax.rem(t, tiles) * TILE
        for plane in range(nz):
            here, rate = rates(
                fine, plane + 1, row + TILE, visc[plane + 1, pl.ds(row, TILE), :], nx)
            for c in range(3):
                coarse = jump[c, plane, pl.ds(row, TILE), :]
                change = here[c] + FINE_STEP * rate[c] - coarse
                jump[c, plane, pl.ds(row, TILE), :] = change
                result[0, c, plane, pl.ds(row, TILE), :] = coarse + change
        return _

    def correct(t, _):
        row = lax.rem(t, tiles) * TILE
        for plane in range(nz):
            here, rate = rates(
                start, plane + 1, row + TILE, visc[plane + 1, pl.ds(row, TILE), :], nx)
            for c in range(3):
                result[0, c, plane, pl.ds(row, TILE), :] = (
                    here[c] + COARSE_STEP * rate[c] + jump[c, plane, pl.ds(row, TILE), :])
        return _

    def hand_on(group):
        if groups > 1 and group:
            @pl.when(turn == 0)
            def _():
                for piece in group:
                    pass_copy(*piece).start()

    def take_over(group):
        if groups > 1 and group:
            @pl.when(turn > 0)
            def _():
                for piece in group:
                    pass_copy(*piece).wait_recv()
                    for copy in edge_copies(*piece):
                        copy.start()

    for k in range(len(chunks)):
        for copy in halos[k]:
            copy.wait_recv()
        last = k == len(chunks) - 1
        if last:
            wrap_rows(field)
        lax.fori_loop(*fine_one[k], first_step, None, unroll=UNROLL)
        if last:
            wrap_rows(fine)
        for piece in numbered[k]:
            lax.fori_loop(piece[1], piece[2], second_step, None, unroll=UNROLL)
            hand_on([piece])
        if groups == 2 and k > 0:
            take_over(numbered[k - 1])

    if groups > 1:
        @pl.when(turn > 0)
        def _():
            for k in range(len(chunks)):
                if groups > 2 or k == len(chunks) - 1:
                    for piece in numbered[k]:
                        pass_copy(*piece).wait_recv()
                        for copy in edge_copies(*piece):
                            copy.start()
            done = 3
            for (_, upto), group in zip(fine_two, numbered):
                for piece in group:
                    for copy in edge_copies(*piece):
                        copy.wait_recv()
                upto = upto + 1 if upto > tiles else upto - 1
                if upto > tiles:
                    wrap_rows(start)
                if upto > done:
                    lax.fori_loop(done, upto, correct, None, unroll=UNROLL)
                    done = upto

            @pl.when(turn < groups - 1)
            def _():
                for group in numbered:
                    for piece in group:
                        pass_copy(*piece).start()

            for group in numbered:
                for piece in group:
                    for copy in edge_copies(*piece):
                        copy.wait_send()

        @pl.when(turn < groups - 1)
        def _():
            for group in numbered:
                for piece in group:
                    pass_copy(*piece).wait_send()

    for copies in halos:
        for copy in copies:
            copy.wait_send()


def local(count, groups, states, viscosity):
    _, _, nz, ny, nx = states.shape
    chunks, _, fine_two = row_plan(ny // TILE)
    passes = sum(len(pieces_of(a, b, ny // TILE)) for a, b in fine_two)
    padded = ny + 2 * TILE
    f32 = jnp.float32
    dma = pltpu.SemaphoreType.DMA
    return pl.pallas_call(
        functools.partial(kernel, count, groups),
        out_shape=pltpu.VMEM(states.shape, f32),
        in_specs=[pl.BlockSpec(memory_space=pl.ANY)] * 2,
        out_specs=pl.BlockSpec(memory_space=pltpu.VMEM),
        scratch_shapes=[
            pltpu.VMEM((3, nz + 4, padded, nx), f32),
            pltpu.VMEM((nz + 2, ny, nx), f32),
            pltpu.VMEM((3, nz + 2, padded, nx), f32),
            pltpu.VMEM((3, nz, ny, nx), f32),
            pltpu.VMEM((3, nz + 2, padded, nx), f32),
            dma((2,)),
            dma((2, len(chunks))),
            dma((2, len(chunks))),
            dma((2, len(chunks))),
            dma((2, len(chunks))),
            dma((passes,)),
            dma((passes,)),
            dma((2, passes)),
            dma((2, passes)),
        ],
        compiler_params=pltpu.CompilerParams(
            collective_id=0, has_side_effects=True),
    )(
        pltpu.with_memory_space_constraint(states, pltpu.HBM),
        pltpu.with_memory_space_constraint(viscosity, pltpu.HBM),
    )


def solution(mesh):
    return jax.shard_map(
        functools.partial(local, mesh.shape["space"], mesh.shape["tm"]),
        mesh=mesh,
        in_specs=(P("tm", None, "space", None, None), P("space", None, None)),
        out_specs=P("tm", None, "space", None, None),
        check_vma=False,
    )
```
